32 devices in a mesh: dom: 32 (over z, y, x, core).
Axes of the slice: x: 2, y: 2, z: 4, core: 2. Of those that a mesh axis runs over, the one named last changes fastest.
Arguments:
- node_feat: float32 [131072, 128], P('dom'), may hold values from -6 to 6
- out_grad: float32 [131072, 128], P('dom'), may hold values from -6 to 6
- lattice_of: int32 [256, 512], P('dom'), may hold values from 0 to 511, each once within a row
- element_place: int32 [32, 8], P('dom'), may hold values from 0 to 7, each once within a row
- edge_in: float32 [256, 128], replicated, may hold values from -0.375 to 0.375
- edge_mid: float32 [2, 128, 128], replicated, may hold values from -0.5 to 0.5
- edge_bias: float32 [3, 128], replicated, may hold values from -3 to 3
- node_in: float32 [256, 128], replicated, may hold values from -0.375 to 0.375
- node_mid: float32 [2, 128, 128], replicated, may hold values from -0.5 to 0.5
- node_bias: float32 [3, 128], replicated, may hold values from -3 to 3
Outputs:
- new_feat: float32 [131072, 128], P('dom')
- feat_grad: float32 [131072, 128], P('dom')
- edge_in_grad: float32 [256, 128], replicated
- edge_mid_grad: float32 [2, 128, 128], replicated
- edge_bias_grad: float32 [3, 128], replicated
- node_in_grad: float32 [256, 128], replicated
- node_mid_grad: float32 [2, 128, 128], replicated
- node_bias_grad: float32 [3, 128], replicated
The draws below stay inside these ranges and needn't reach their ends.
Inputs may be any that keep to these rules, and one draw needn't show every extreme that they name: `lattice_of`: row s lists, for node k of element slot s, its lattice point x * 8 * 8 + y * 8 + z; every row is a permutation. `element_place`: row d lists, for each element slot of partition d, its place p in the partition's 2 x 2 x 2 block of elements, at offset (p // 4, p // 2 % 2, p % 2) in elements; every row is a permutation.
All inputs are finite; a program needn't handle non-finite values.
Results may differ from the reference program's by a relative error of at most 0.0003.
Values sent between devices are 32-bit elements; how exact they have to be, the bound alone decides.
A program may use at most 128 MiB of HBM per device.

```python
import math
import jax
import jax.numpy as jnp
from jax import lax

H = 128
SIDE = 8
ELEM_DEV = 8
DGX = 4
DGY = 4
NODES_EL = 512
ELEMS = 256
NODES = 131072
N_DOM = 32


def levels(key, dims, cuts, least, largest):
    gain = 1.0
    for axis_at, shards_of in cuts:
        draws = jax.random.uniform(jax.random.fold_in(jax.random.fold_in(key, 6), axis_at), (shards_of,), jnp.float32, least / len(cuts), largest / len(cuts))
        gain = gain * jnp.repeat(jnp.exp(draws), dims[axis_at] // shards_of).reshape((-1,) + (1,) * (len(dims) - 1 - axis_at))
    return gain


def bell_draw(rng, dims, scale, limit, split=(), kind=jnp.bfloat16):
    entries = scale * jax.random.normal(rng, dims, jnp.float32)
    if split:
        entries = entries * levels(rng, dims, split, -0.22, 0.18)
    return jnp.clip(entries, -limit, limit).astype(kind)


def setup_inputs(seed: int = 0) -> dict:
    key_of = jax.random.split(jax.random.key(seed), 11)
    return {
        "node_feat": bell_draw(key_of[0], (NODES, H), 1.0, 6.0, ((0, 32),), jnp.float32),
        "out_grad": bell_draw(key_of[1], (NODES, H), 1.0, 6.0, ((0, 32),), jnp.float32),
        "lattice_of": jax.vmap(lambda own: jax.random.permutation(own, NODES_EL))(jax.random.split(key_of[2], ELEMS)).reshape((ELEMS, NODES_EL)).astype(jnp.int32),
        "element_place": jax.vmap(lambda own: jax.random.permutation(own, ELEM_DEV))(jax.random.split(key_of[3], N_DOM)).reshape((N_DOM, ELEM_DEV)).astype(jnp.int32),
        "edge_in": bell_draw(key_of[4], (2 * H, H), (2 * H) ** -0.5, 0.375, (), jnp.float32),
        "edge_mid": bell_draw(key_of[5], (2, H, H), H ** -0.5, 0.5, (), jnp.float32),
        "edge_bias": bell_draw(key_of[6], (3, H), 0.5, 3.0, (), jnp.float32),
        "node_in": bell_draw(key_of[7], (2 * H, H), (2 * H) ** -0.5, 0.375, (), jnp.float32),
        "node_mid": bell_draw(key_of[8], (2, H, H), H ** -0.5, 0.5, (), jnp.float32),
        "node_bias": bell_draw(key_of[9], (3, H), 0.5, 3.0, (), jnp.float32),
    }


highest = lax.Precision.HIGHEST

def matmul(values, weight):
    flat = values.reshape(-1, values.shape[-1])
    result = jnp.dot(flat, weight, precision=highest, preferred_element_type=jnp.float32)
    return result.reshape(values.shape[:-1] + (weight.shape[1],))

def edge_messages(lattice, edge_in, edge_mid, edge_bias):
    channels = lattice.shape[-1]
    extent = lattice.shape[1]
    toward = matmul(lattice, edge_in[:channels])
    source = matmul(lattice, edge_in[channels:])
    summed = jnp.zeros_like(lattice)
    for spatial in (1, 2, 3):
        for upward in (True, False):
            if upward:
                target = lax.slice_in_dim(toward, 0, extent - 1, axis=spatial)
                anchor = lax.slice_in_dim(source, 1, extent, axis=spatial)
                padding = (0, 1)
            else:
                target = lax.slice_in_dim(toward, 1, extent, axis=spatial)
                anchor = lax.slice_in_dim(source, 0, extent - 1, axis=spatial)
                padding = (1, 0)
            hidden = jax.nn.silu(target + anchor + edge_bias[0])
            hidden = jax.nn.silu(matmul(hidden, edge_mid[0]) + edge_bias[1])
            message = matmul(hidden, edge_mid[1]) + edge_bias[2]
            widths = [(0, 0)] * 5
            widths[spatial] = padding
            summed = summed + jnp.pad(message, widths)
    return summed

def node_update(lattice, gathered, node_in, node_mid, node_bias):
    channels = lattice.shape[-1]
    hidden = jax.nn.silu(matmul(lattice, node_in[:channels]) + matmul(gathered, node_in[channels:]) + node_bias[0])
    hidden = jax.nn.silu(matmul(hidden, node_mid[0]) + node_bias[1])
    return lattice + matmul(hidden, node_mid[1]) + node_bias[2]

def to_lattice(node_rows, lattice_of):
    channels = node_rows.shape[-1]
    count = lattice_of.shape[0]
    blocks = node_rows.reshape(count, -1, channels)
    placed = jax.vmap(lambda values, ordering: jnp.zeros_like(values).at[ordering].set(values))(blocks, lattice_of)
    return placed.reshape(count, SIDE, SIDE, SIDE, channels)

def from_lattice(lattice, lattice_of):
    channels = lattice.shape[-1]
    count = lattice_of.shape[0]
    blocks = lattice.reshape(count, -1, channels)
    picked = jax.vmap(lambda values, ordering: values[ordering])(blocks, lattice_of)
    return picked.reshape(-1, channels)

def block_corner(element_place, global_slot):
    device = global_slot // ELEM_DEV
    slot = global_slot % ELEM_DEV
    offset = element_place[device, slot].astype(jnp.int32)
    grid_x = device % DGX
    grid_y = device // DGX % DGY
    grid_z = device // (DGX * DGY)
    stride = SIDE - 1
    corner_x = ((2 * grid_x + offset // 4) * stride).astype(jnp.int32)
    corner_y = ((2 * grid_y + offset // 2 % 2) * stride).astype(jnp.int32)
    corner_z = ((2 * grid_z + offset % 2) * stride).astype(jnp.int32)
    return (corner_x, corner_y, corner_z, jnp.zeros((), jnp.int32))

def consistent(summed, element_place):
    channels = summed.shape[-1]
    flat = summed.reshape((-1, SIDE, SIDE, SIDE, channels))
    total = flat.shape[0]
    depth = N_DOM // (DGX * DGY)
    extent = 2 * (SIDE - 1)
    field = jnp.zeros((DGX * extent + 1, DGY * extent + 1, depth * extent + 1, channels), summed.dtype)
    sizes = (SIDE, SIDE, SIDE, channels)

    def add_one(global_slot, field):
        global_slot = jnp.asarray(global_slot).astype(jnp.int32)
        start = block_corner(element_place, global_slot)
        current = lax.dynamic_slice(field, start, sizes)
        return lax.dynamic_update_slice(field, current + flat[global_slot], start)
    field = lax.fori_loop(0, total, add_one, field)

    def take_one(global_slot):
        return lax.dynamic_slice(field, block_corner(element_place, global_slot), sizes)
    return lax.map(take_one, jnp.arange(total, dtype=jnp.int32)).reshape(summed.shape)

def reference(node_feat, out_grad, lattice_of, element_place, edge_in, edge_mid, edge_bias, node_in, node_mid, node_bias):
    channels = node_feat.shape[-1]
    shaped = (N_DOM, ELEM_DEV, SIDE, SIDE, SIDE, channels)
    lattice = to_lattice(node_feat, lattice_of).reshape(shaped)
    cotangent = to_lattice(out_grad, lattice_of).reshape(shaped)
    summed = lax.map(lambda block: edge_messages(block, edge_in, edge_mid, edge_bias), lattice)
    gathered = consistent(summed, element_place)
    updated = lax.map(lambda pair: node_update(pair[0], pair[1], node_in, node_mid, node_bias), (lattice, gathered))

    def node_back(triple):
        block, around, incoming = triple
        _, pullback = jax.vjp(node_update, block, around, node_in, node_mid, node_bias)
        return pullback(incoming)
    direct_grad, around_grad, node_in_grad, node_mid_grad, node_bias_grad = lax.map(node_back, (lattice, gathered, cotangent))
    around_total = consistent(around_grad, element_place)

    def edge_back(pair):
        block, incoming = pair
        _, pullback = jax.vjp(edge_messages, block, edge_in, edge_mid, edge_bias)
        return pullback(incoming)
    edge_grad, edge_in_grad, edge_mid_grad, edge_bias_grad = lax.map(edge_back, (lattice, around_total))
    scale = 1.0 / math.sqrt(NODES)
    flat_shape = (-1, SIDE, SIDE, SIDE, channels)
    new_feat = from_lattice(updated.reshape(flat_shape), lattice_of)
    feat_grad = from_lattice((direct_grad + edge_grad).reshape(flat_shape), lattice_of)
    return (new_feat, feat_grad, lax.optimization_barrier(jnp.sum(edge_in_grad, 0)) * scale, lax.optimization_barrier(jnp.sum(edge_mid_grad, 0)) * scale, lax.optimization_barrier(jnp.sum(edge_bias_grad, 0)) * scale, lax.optimization_barrier(jnp.sum(node_in_grad, 0)) * scale, lax.optimization_barrier(jnp.sum(node_mid_grad, 0)) * scale, lax.optimization_barrier(jnp.sum(node_bias_grad, 0)) * scale)
```

```python
import functools
import math

import jax
import jax.numpy as jnp
from jax import lax
from jax.experimental import pallas as pl
from jax.experimental.pallas import tpu as pltpu
from jax.sharding import PartitionSpec as P

SIDE = 8
ELEM_DEV = 8
DGX = 4
DGY = 4
NODES_EL = 512

F32 = jnp.float32
BF16 = jnp.bfloat16
VMEM_BYTES = 48 * 2**20
PAIRS = ((2, True), (2, False), (0, True), (0, False), (1, True), (1, False))


def split(values):
    high = values.astype(BF16)
    low = (values - high.astype(F32)).astype(BF16)
    return jnp.concatenate([high, low], axis=1)


def spread(weight):
    halves = split(weight)
    return jnp.concatenate([halves, halves], axis=0)


def times(pair, spread_weight):
    wide = jnp.dot(pair, spread_weight, preferred_element_type=F32)
    half = wide.shape[1] // 2
    return wide[:, :half] + wide[:, half:]


def across(left, right):
    wide = lax.dot_general(left, right, (((0,), (0,)), ((), ())), preferred_element_type=F32)
    m, n = wide.shape[0] // 2, wide.shape[1] // 2
    return (wide[:m, :n] + wide[m:, n:]) + (wide[:m, n:] + wide[m:, :n])


def column_sum(values):
    return jnp.sum(values, axis=0, keepdims=True)


def one_hot(order):
    n = order.shape[1]
    points = lax.broadcasted_iota(jnp.int32, (n, n), 0)
    return jnp.where(points == order, 1.0, 0.0).astype(BF16)


def place_rows(hot, values):
    wide = jnp.dot(hot, split(values), preferred_element_type=F32)
    half = wide.shape[1] // 2
    return wide[:, :half] + wide[:, half:]


def pick_rows(hot, values):
    wide = lax.dot_general(hot, split(values), (((0,), (0,)), ((), ())), preferred_element_type=F32)
    half = wide.shape[1] // 2
    return wide[:, :half] + wide[:, half:]


def slope(half_value, tanh):
    return (1.0 + tanh) * (1.0 + half_value * (1.0 - tanh))


def window(axis, first):
    index = [slice(None)] * 3
    if axis != 2:
        index[axis] = slice(0, SIDE - 1) if first else slice(1, SIDE)
    return tuple(index)


def rows_of(ref, axis, first):
    picked = ref[window(axis, first)]
    return picked.reshape(-1, picked.shape[-1])


def rolled(rows, shift):
    grouped = rows.reshape(-1, SIDE, rows.shape[-1])
    return pltpu.roll(grouped, shift % SIDE, 1).reshape(rows.shape)


def add_rows(ref, axis, first, rows):
    index = window(axis, first)
    ref[index] += rows.reshape(ref[index].shape)


def inner(rows, channels, upward):
    z = lax.broadcasted_iota(jnp.int32, (rows, channels), 0) % SIDE
    return z < SIDE - 1 if upward else z > 0


def degree(rows, channels):
    at = lax.broadcasted_iota(jnp.int32, (rows, channels), 0)
    total = jnp.zeros((rows, channels), F32)
    for coordinate in (at // (SIDE * SIDE), at // SIDE % SIDE, at % SIDE):
        edge = (coordinate == 0) | (coordinate == SIDE - 1)
        total = total + jnp.where(edge, 1.0, 2.0)
    return total


def senders(source, axis, upward):
    if axis == 2:
        whole = source[...].reshape(-1, source.shape[-1])
        return rolled(whole, -1 if upward else 1)
    return rows_of(source, axis, not upward)


def edge_forward_kernel(
    place, feat, order, w_in, w_mid, bias,
    lattice_out, summed_out, local_out,
    toward, source, total, w_toward, w_source, w_hidden, w_last,
):
    channels = feat.shape[1]

    @pl.when(pl.program_id(0) == 0)
    def _():
        w_toward[...] = spread(0.5 * w_in[:channels])
        w_source[...] = spread(0.5 * w_in[channels:])
        w_hidden[...] = spread(0.5 * w_mid[0])
        w_last[...] = spread(w_mid[1])

    lattice = place_rows(one_hot(order[0]), feat[...])
    lattice_out[...] = lattice
    pair = split(lattice)
    shape = toward.shape
    toward[...] = (times(pair, w_toward[...]) + 0.5 * bias[0:1]).reshape(shape)
    source[...] = times(pair, w_source[...]).reshape(shape)
    bias_half = 0.5 * bias[1:2]
    for axis, upward in PAIRS:
        y = rows_of(toward, axis, upward) + senders(source, axis, upward)
        hidden = y + y * jnp.tanh(y)
        y = times(split(hidden), w_hidden[...]) + bias_half
        hidden = y + y * jnp.tanh(y)
        if axis == 2:
            hidden = jnp.where(inner(*hidden.shape, upward), hidden, 0.0)
        if (axis, upward) == PAIRS[0]:
            total[...] = hidden.reshape(shape)
        else:
            add_rows(total, axis, upward, hidden)
    summed = total[...].reshape(lattice.shape)
    summed_out[...] = summed
    local_out[...] = times(split(summed), w_last[...]) + degree(*lattice.shape) * bias[2:3]


def node_kernel(
    place, lattice_ref, gathered_ref, cotangent, order, w_in, w_mid, bias,
    new_out, direct_out, around_out, grads,
    w_own, w_near, w_hidden, w_last, b_own, b_near, b_hidden, b_last,
):
    channels = lattice_ref.shape[1]

    @pl.when(pl.program_id(0) == 0)
    def _():
        w_own[...] = spread(0.5 * w_in[:channels])
        w_near[...] = spread(0.5 * w_in[channels:])
        w_hidden[...] = spread(0.5 * w_mid[0])
        w_last[...] = spread(w_mid[1])
        b_own[...] = spread(w_in[:channels].T)
        b_near[...] = spread(w_in[channels:].T)
        b_hidden[...] = spread(0.5 * w_mid[0].T)
        b_last[...] = spread(0.5 * w_mid[1].T)
        grads[...] = jnp.zeros(grads.shape, F32)

    hot = one_hot(order[0])
    lattice = lattice_ref[...]
    own = split(lattice)
    near = split(gathered_ref[...])
    y1 = times(own, w_own[...]) + times(near, w_near[...]) + 0.5 * bias[0:1]
    t1 = jnp.tanh(y1)
    hidden1 = split(y1 + y1 * t1)
    y2 = times(hidden1, w_hidden[...]) + 0.5 * bias[1:2]
    t2 = jnp.tanh(y2)
    hidden2 = split(y2 + y2 * t2)
    new_out[...] = pick_rows(hot, lattice + times(hidden2, w_last[...]) + bias[2:3])

    incoming = place_rows(hot, cotangent[...])
    incoming_pair = split(incoming)
    back2 = times(incoming_pair, b_last[...]) * slope(y2, t2)
    back2_pair = split(back2)
    back1 = times(back2_pair, b_hidden[...]) * slope(y1, t1)
    back1_pair = split(back1)
    direct_out[...] = incoming + times(back1_pair, b_own[...])
    around_out[...] = times(back1_pair, b_near[...])
    c = channels
    grads[0:c] += across(own, back1_pair)
    grads[c:2 * c] += across(near, back1_pair)
    grads[2 * c:3 * c] += across(hidden1, back2_pair)
    grads[3 * c:4 * c] += across(hidden2, incoming_pair)
    grads[4 * c:4 * c + 1] += column_sum(back1)
    grads[4 * c + 1:4 * c + 2] += column_sum(back2)
    grads[4 * c + 2:4 * c + 3] += column_sum(incoming)


def edge_backward_kernel(
    place, lattice_ref, around_ref, summed_ref, direct_ref, order, w_in, w_mid, bias,
    feat_out, grads,
    toward, source, incoming, to_toward, to_source, left, right,
    w_toward, w_source, w_hidden, b_toward, b_source, b_hidden, b_last,
):
    channels = lattice_ref.shape[1]
    c = channels

    @pl.when(pl.program_id(0) == 0)
    def _():
        w_toward[...] = spread(0.5 * w_in[:channels])
        w_source[...] = spread(0.5 * w_in[channels:])
        w_hidden[...] = spread(0.5 * w_mid[0])
        b_toward[...] = spread(w_in[:channels].T)
        b_source[...] = spread(w_in[channels:].T)
        b_hidden[...] = spread(0.5 * w_mid[0].T)
        b_last[...] = spread(0.5 * w_mid[1].T)
        grads[...] = jnp.zeros(grads.shape, F32)

    around = around_ref[...]
    around_pair = split(around)
    shape = toward.shape
    pair = split(lattice_ref[...])
    toward[...] = (times(pair, w_toward[...]) + 0.5 * bias[0:1]).reshape(shape)
    source[...] = times(pair, w_source[...]).reshape(shape)
    incoming[...] = times(around_pair, b_last[...]).reshape(shape)
    bias_half = 0.5 * bias[1:2]
    back2_sum = jnp.zeros((1, channels), F32)
    start = 0
    for axis, upward in PAIRS:
        y1 = rows_of(toward, axis, upward) + senders(source, axis, upward)
        rows = y1.shape[0]
        span = slice(start, start + rows)
        start += rows
        t1 = jnp.tanh(y1)
        hidden_pair = split(y1 + y1 * t1)
        left[span] = hidden_pair
        y2 = times(hidden_pair, w_hidden[...]) + bias_half
        t2 = jnp.tanh(y2)
        arrived = rows_of(incoming, axis, upward)
        if axis == 2:
            arrived = jnp.where(inner(*arrived.shape, upward), arrived, 0.0)
        back2 = arrived * slope(y2, t2)
        back2_sum = back2_sum + column_sum(back2)
        back2_pair = split(back2)
        right[span] = back2_pair
        back1 = times(back2_pair, b_hidden[...]) * slope(y1, t1)
        sent = rolled(back1, 1 if upward else -1) if axis == 2 else back1
        if (axis, upward) == PAIRS[0]:
            to_toward[...] = back1.reshape(shape)
            to_source[...] = sent.reshape(shape)
        else:
            add_rows(to_toward, axis, upward, back1)
            add_rows(to_source, axis, not upward, sent)
    back_toward = to_toward[...].reshape(around.shape)
    toward_pair = split(back_toward)
    source_pair = split(to_source[...].reshape(around.shape))
    total = direct_ref[...] + times(toward_pair, b_toward[...]) + times(source_pair, b_source[...])
    feat_out[...] = pick_rows(one_hot(order[0]), total)
    grads[0:c] += across(pair, toward_pair)
    grads[c:2 * c] += across(pair, source_pair)
    grads[2 * c:3 * c] += across(left[...], right[...])
    grads[3 * c:4 * c] += across(split(summed_ref[...]), around_pair)
    grads[4 * c:4 * c + 1] += column_sum(back_toward)
    grads[4 * c + 1:4 * c + 2] += back2_sum
    grads[4 * c + 2:4 * c + 3] += column_sum(around * degree(*around.shape))


def slot_at(place, at):
    slot = jnp.int32(0)
    for s in range(ELEM_DEV):
        slot = slot + jnp.where(place[0, s] == at, jnp.int32(s), jnp.int32(0))
    return slot


def on_elements(kernel, place, arrays, slotted, weights, order, out_rows, out_slotted, grads, scratch, cost):
    channels = arrays[0].shape[1]
    by_slot = pl.BlockSpec((NODES_EL, channels), lambda p, place: (slot_at(place, p), 0))
    by_place = pl.BlockSpec((NODES_EL, channels), lambda p, place: (p, 0))

    def whole(array):
        zeros = (0,) * array.ndim
        return pl.BlockSpec(array.shape, lambda p, place: zeros)

    order3 = order.reshape(order.shape[0], 1, order.shape[1])
    in_specs = [by_slot if s else by_place for s in slotted]
    in_specs.append(pl.BlockSpec((1, 1, order.shape[1]), lambda p, place: (slot_at(place, p), 0, 0)))
    in_specs += [whole(w) for w in weights]
    rows = order.shape[0] * NODES_EL
    out_shape = [jax.ShapeDtypeStruct((rows, channels), F32) for _ in range(out_rows)]
    out_specs = [by_slot if s else by_place for s in out_slotted]
    if grads:
        total = jax.ShapeDtypeStruct((4 * channels + SIDE, channels), F32)
        out_shape.append(total)
        out_specs.append(whole(total))
    return pl.pallas_call(
        kernel,
        grid_spec=pltpu.PrefetchScalarGridSpec(
            num_scalar_prefetch=1,
            grid=(order.shape[0],),
            in_specs=in_specs,
            out_specs=out_specs,
            scratch_shapes=scratch,
        ),
        out_shape=out_shape,
        cost_estimate=cost,
        compiler_params=pltpu.CompilerParams(
            dimension_semantics=("arbitrary",), vmem_limit_bytes=VMEM_BYTES
        ),
    )(place, *arrays, order3, *weights)


def plane(axis, element, side):
    base = element * NODES_EL
    far = (SIDE - 1) * side
    if axis == 0:
        return [(pl.ds(base + far * SIDE * SIDE, SIDE * SIDE), SIDE * SIDE)]
    if axis == 1:
        return [(pl.ds(base + x * SIDE * SIDE + far * SIDE, SIDE), SIDE) for x in range(SIDE)]
    return [(pl.ds(base + far, SIDE * SIDE, stride=SIDE), SIDE * SIDE)]


def exchange_kernel(devices, field_in, field, outgoing, arriving, send_sem, recv_sem):
    me = lax.axis_index("dom")
    depth = devices // (DGX * DGY)
    grid = (me % DGX, me // DGX % DGY, me // (DGX * DGY))
    limits = (DGX, DGY, depth)
    strides = (1, DGX, DGX * DGY)
    exists = []
    partner = []
    for axis in range(3):
        exists.append((grid[axis] > 0, grid[axis] < limits[axis] - 1))
        partner.append(
            (
                jnp.where(exists[axis][0], me - strides[axis], me + strides[axis]),
                jnp.where(exists[axis][1], me + strides[axis], me - strides[axis]),
            )
        )
    barrier = pltpu.get_barrier_semaphore()
    for axis in range(3):
        for side in range(2):

            @pl.when(exists[axis][side])
            def _():
                pl.semaphore_signal(
                    barrier, inc=1, device_id=(partner[axis][side],), device_id_type=pl.DeviceIdType.MESH
                )

    field[...] = field_in[...]
    peers = jnp.int32(0)
    for axis in range(3):
        for side in range(2):
            peers = peers + jnp.where(exists[axis][side], jnp.int32(1), jnp.int32(0))
    pl.semaphore_wait(barrier, peers)
    for axis in (2, 1, 0):
        weight = (4, 2, 1)[axis]
        sides = [[p for p in range(ELEM_DEV) if p // weight % 2 == side] for side in range(2)]
        copies = []
        for side in range(2):
            at = 0
            for element in sides[side]:
                for rows, count in plane(axis, element, side):
                    outgoing[axis, side, at:at + count] = field[rows]
                    at += count
            copies.append(
                pltpu.make_async_remote_copy(
                    src_ref=outgoing.at[axis, side],
                    dst_ref=arriving.at[axis, 1 - side],
                    send_sem=send_sem.at[axis, side],
                    recv_sem=recv_sem.at[axis, 1 - side],
                    device_id=(partner[axis][side],),
                    device_id_type=pl.DeviceIdType.MESH,
                )
            )
        for side in range(2):

            @pl.when(exists[axis][side])
            def _():
                copies[side].start()

        for lower, upper in zip(*sides):
            for (rows_l, _), (rows_u, _) in zip(plane(axis, lower, 1), plane(axis, upper, 0)):
                both = field[rows_l] + field[rows_u]
                field[rows_l] = both
                field[rows_u] = both
        for side in range(2):

            @pl.when(exists[axis][side])
            def _():
                copies[1 - side].wait_recv()
                at = 0
                for element in sides[side]:
                    for rows, count in plane(axis, element, side):
                        field[rows] += arriving[axis, side, at:at + count]
                        at += count
                copies[side].wait_send()


def make_consistent(field, collective):
    devices = lax.axis_size("dom")
    face = ELEM_DEV // 2 * SIDE * SIDE
    channels = field.shape[1]
    return pl.pallas_call(
        functools.partial(exchange_kernel, devices),
        out_shape=jax.ShapeDtypeStruct(field.shape, F32),
        in_specs=[pl.BlockSpec(memory_space=pltpu.VMEM)],
        out_specs=pl.BlockSpec(memory_space=pltpu.VMEM),
        scratch_shapes=[
            pltpu.VMEM((3, 2, face, channels), F32),
            pltpu.VMEM((3, 2, face, channels), F32),
            pltpu.SemaphoreType.DMA((3, 2)),
            pltpu.SemaphoreType.DMA((3, 2)),
        ],
        compiler_params=pltpu.CompilerParams(
            collective_id=collective, has_side_effects=True, vmem_limit_bytes=VMEM_BYTES
        ),
    )(field)


def unpack(total, scale):
    channels = total.shape[1]
    c = channels
    total = total * scale
    return total[:2 * c], total[2 * c:4 * c].reshape(2, c, c), total[4 * c:4 * c + 3]


def body(
    node_feat,
    out_grad,
    lattice_of,
    element_place,
    edge_in,
    edge_mid,
    edge_bias,
    node_in,
    node_mid,
    node_bias,
):
    channels = node_feat.shape[1]
    cube = pltpu.VMEM((SIDE, SIDE, SIDE, channels), F32)
    wide = pltpu.VMEM((2 * channels, 2 * channels), BF16)
    pairs = 4 * (NODES_EL - SIDE * SIDE) + 2 * NODES_EL
    edge = (edge_in, edge_mid, edge_bias)
    node = (node_in, node_mid, node_bias)

    def cost(rows):
        return pl.CostEstimate(
            flops=8 * rows * channels * channels * lattice_of.shape[0],
            bytes_accessed=16 * node_feat.size,
            transcendentals=0,
        )

    lattice, summed, local = on_elements(
        edge_forward_kernel, element_place, [node_feat], [True], edge, lattice_of,
        3, [False] * 3, False, [cube] * 3 + [wide] * 4, cost(pairs),
    )
    gathered = make_consistent(local, 0)
    new_feat, direct, around, node_total = on_elements(
        node_kernel, element_place, [lattice, gathered, out_grad], [False, False, True], node, lattice_of,
        3, [True, False, False], True, [wide] * 8, cost(12 * NODES_EL),
    )
    around = make_consistent(around, 1)
    node_total = lax.psum(node_total, "dom")
    tall = pltpu.VMEM((pairs, 2 * channels), BF16)
    feat_grad, edge_total = on_elements(
        edge_backward_kernel, element_place, [lattice, around, summed, direct], [False] * 4, edge, lattice_of,
        1, [True], True, [cube] * 5 + [tall] * 2 + [wide] * 7, cost(3 * pairs),
    )
    edge_total = lax.psum(edge_total, "dom")
    scale = 1.0 / math.sqrt(lax.axis_size("dom") * ELEM_DEV * NODES_EL)
    return (new_feat, feat_grad) + unpack(edge_total, scale) + unpack(node_total, scale)


def solution(mesh):
    in_specs = (
        P("dom", None),
        P("dom", None),
        P("dom", None),
        P("dom", None),
        P(),
        P(),
        P(),
        P(),
        P(),
        P(),
    )
    out_specs = (P("dom", None), P("dom", None), P(), P(), P(), P(), P(), P())
    return jax.shard_map(body, mesh=mesh, in_specs=in_specs, out_specs=out_specs, check_vma=False)
```

```python
import functools
import math

import jax
import jax.numpy as jnp
from jax import lax
from jax.experimental import pallas as pl
from jax.experimental.pallas import tpu as pltpu
from jax.sharding import PartitionSpec as P

SIDE = 8
ELEM_DEV = 8
DGX = 4
DGY = 4
NODES_EL = 512

F32 = jnp.float32
BF16 = jnp.bfloat16
VMEM_BYTES = 48 * 2**20
PAIRS = ((2, True), (2, False), (0, True), (0, False), (1, True), (1, False))


def split(values):
    high = values.astype(BF16)
    low = (values - high.astype(F32)).astype(BF16)
    return jnp.concatenate([high, low], axis=1)


def spread(weight):
    halves = split(weight)
    return jnp.concatenate([halves, halves], axis=0)


def times(pair, spread_weight):
    wide = jnp.dot(pair, spread_weight, preferred_element_type=F32)
    half = wide.shape[1] // 2
    return wide[:, :half] + wide[:, half:]


def across(left, right):
    wide = lax.dot_general(left, right, (((0,), (0,)), ((), ())), preferred_element_type=F32)
    m, n = wide.shape[0] // 2, wide.shape[1] // 2
    return (wide[:m, :n] + wide[m:, n:]) + (wide[:m, n:] + wide[m:, :n])


def column_sum(values):
    return jnp.sum(values, axis=0, keepdims=True)


def one_hot(order):
    n = order.shape[1]
    points = lax.broadcasted_iota(jnp.int32, (n, n), 0)
    return jnp.where(points == order, 1.0, 0.0).astype(BF16)


def place_rows(hot, values):
    wide = jnp.dot(hot, split(values), preferred_element_type=F32)
    half = wide.shape[1] // 2
    return wide[:, :half] + wide[:, half:]


def pick_rows(hot, values):
    wide = lax.dot_general(hot, split(values), (((0,), (0,)), ((), ())), preferred_element_type=F32)
    half = wide.shape[1] // 2
    return wide[:, :half] + wide[:, half:]


def slope(half_value, tanh):
    return (1.0 + tanh) * (1.0 + half_value * (1.0 - tanh))


def window(axis, first):
    index = [slice(None)] * 3
    if axis != 2:
        index[axis] = slice(0, SIDE - 1) if first else slice(1, SIDE)
    return tuple(index)


def rows_of(ref, axis, first):
    picked = ref[window(axis, first)]
    return picked.reshape(-1, picked.shape[-1])


def rolled(rows, shift):
    grouped = rows.reshape(-1, SIDE, rows.shape[-1])
    return pltpu.roll(grouped, shift % SIDE, 1).reshape(rows.shape)


def add_rows(ref, axis, first, rows):
    index = window(axis, first)
    ref[index] += rows.reshape(ref[index].shape)


def inner(rows, channels, upward):
    z = lax.broadcasted_iota(jnp.int32, (rows, channels), 0) % SIDE
    return z < SIDE - 1 if upward else z > 0


def degree(rows, channels):
    at = lax.broadcasted_iota(jnp.int32, (rows, channels), 0)
    total = jnp.zeros((rows, channels), F32)
    for coordinate in (at // (SIDE * SIDE), at // SIDE % SIDE, at % SIDE):
        edge = (coordinate == 0) | (coordinate == SIDE - 1)
        total = total + jnp.where(edge, 1.0, 2.0)
    return total


def senders(source, axis, upward):
    if axis == 2:
        whole = source[...].reshape(-1, source.shape[-1])
        return rolled(whole, -1 if upward else 1)
    return rows_of(source, axis, not upward)


def edge_forward_kernel(
    place, feat, order, w_in, w_mid, bias,
    lattice_out, summed_out, local_out,
    toward, source, total, w_toward, w_source, w_hidden, w_last,
):
    channels = feat.shape[1]

    @pl.when(pl.program_id(0) == 0)
    def _():
        w_toward[...] = spread(0.5 * w_in[:channels])
        w_source[...] = spread(0.5 * w_in[channels:])
        w_hidden[...] = spread(0.5 * w_mid[0])
        w_last[...] = spread(w_mid[1])

    lattice = place_rows(one_hot(order[0]), feat[...])
    lattice_out[...] = lattice
    pair = split(lattice)
    shape = toward.shape
    toward[...] = (times(pair, w_toward[...]) + 0.5 * bias[0:1]).reshape(shape)
    source[...] = times(pair, w_source[...]).reshape(shape)
    bias_half = 0.5 * bias[1:2]
    for axis, upward in PAIRS:
        y = rows_of(toward, axis, upward) + senders(source, axis, upward)
        hidden = y + y * jnp.tanh(y)
        y = times(split(hidden), w_hidden[...]) + bias_half
        hidden = y + y * jnp.tanh(y)
        if axis == 2:
            hidden = jnp.where(inner(*hidden.shape, upward), hidden, 0.0)
        if (axis, upward) == PAIRS[0]:
            total[...] = hidden.reshape(shape)
        else:
            add_rows(total, axis, upward, hidden)
    summed = total[...].reshape(lattice.shape)
    summed_out[...] = summed
    local_out[...] = times(split(summed), w_last[...]) + degree(*lattice.shape) * bias[2:3]


def node_kernel(
    place, lattice_ref, gathered_ref, cotangent, order, w_in, w_mid, bias,
    new_out, direct_out, around_out, grads,
    w_own, w_near, w_hidden, w_last, b_own, b_near, b_hidden, b_last,
):
    channels = lattice_ref.shape[1]

    @pl.when(pl.program_id(0) == 0)
    def _():
        w_own[...] = spread(0.5 * w_in[:channels])
        w_near[...] = spread(0.5 * w_in[channels:])
        w_hidden[...] = spread(0.5 * w_mid[0])
        w_last[...] = spread(w_mid[1])
        b_own[...] = spread(w_in[:channels].T)
        b_near[...] = spread(w_in[channels:].T)
        b_hidden[...] = spread(0.5 * w_mid[0].T)
        b_last[...] = spread(0.5 * w_mid[1].T)
        grads[...] = jnp.zeros(grads.shape, F32)

    hot = one_hot(order[0])
    lattice = lattice_ref[...]
    own = split(lattice)
    near = split(gathered_ref[...])
    y1 = times(own, w_own[...]) + times(near, w_near[...]) + 0.5 * bias[0:1]
    t1 = jnp.tanh(y1)
    hidden1 = split(y1 + y1 * t1)
    y2 = times(hidden1, w_hidden[...]) + 0.5 * bias[1:2]
    t2 = jnp.tanh(y2)
    hidden2 = split(y2 + y2 * t2)
    new_out[...] = pick_rows(hot, lattice + times(hidden2, w_last[...]) + bias[2:3])

    incoming = place_rows(hot, cotangent[...])
    incoming_pair = split(incoming)
    back2 = times(incoming_pair, b_last[...]) * slope(y2, t2)
    back2_pair = split(back2)
    back1 = times(back2_pair, b_hidden[...]) * slope(y1, t1)
    back1_pair = split(back1)
    direct_out[...] = incoming + times(back1_pair, b_own[...])
    around_out[...] = times(back1_pair, b_near[...])
    c = channels
    grads[0:c] += across(own, back1_pair)
    grads[c:2 * c] += across(near, back1_pair)
    grads[2 * c:3 * c] += across(hidden1, back2_pair)
    grads[3 * c:4 * c] += across(hidden2, incoming_pair)
    grads[4 * c:4 * c + 1] += column_sum(back1)
    grads[4 * c + 1:4 * c + 2] += column_sum(back2)
    grads[4 * c + 2:4 * c + 3] += column_sum(incoming)


def edge_backward_kernel(
    place, lattice_ref, around_ref, summed_ref, direct_ref, order, w_in, w_mid, bias,
    feat_out, grads,
    toward, source, incoming, to_toward, to_source, left, right,
    w_toward, w_source, w_hidden, b_toward, b_source, b_hidden, b_last,
):
    channels = lattice_ref.shape[1]
    c = channels

    @pl.when(pl.program_id(0) == 0)
    def _():
        w_toward[...] = spread(0.5 * w_in[:channels])
        w_source[...] = spread(0.5 * w_in[channels:])
        w_hidden[...] = spread(0.5 * w_mid[0])
        b_toward[...] = spread(w_in[:channels].T)
        b_source[...] = spread(w_in[channels:].T)
        b_hidden[...] = spread(0.5 * w_mid[0].T)
        b_last[...] = spread(0.5 * w_mid[1].T)
        grads[...] = jnp.zeros(grads.shape, F32)

    around = around_ref[...]
    around_pair = split(around)
    shape = toward.shape
    pair = split(lattice_ref[...])
    toward[...] = (times(pair, w_toward[...]) + 0.5 * bias[0:1]).reshape(shape)
    source[...] = times(pair, w_source[...]).reshape(shape)
    incoming[...] = times(around_pair, b_last[...]).reshape(shape)
    bias_half = 0.5 * bias[1:2]
    back2_sum = jnp.zeros((1, channels), F32)
    start = 0
    for axis, upward in PAIRS:
        y1 = rows_of(toward, axis, upward) + senders(source, axis, upward)
        rows = y1.shape[0]
        span = slice(start, start + rows)
        start += rows
        t1 = jnp.tanh(y1)
        hidden_pair = split(y1 + y1 * t1)
        left[span] = hidden_pair
        y2 = times(hidden_pair, w_hidden[...]) + bias_half
        t2 = jnp.tanh(y2)
        arrived = rows_of(incoming, axis, upward)
        if axis == 2:
            arrived = jnp.where(inner(*arrived.shape, upward), arrived, 0.0)
        back2 = arrived * slope(y2, t2)
        back2_sum = back2_sum + column_sum(back2)
        back2_pair = split(back2)
        right[span] = back2_pair
        back1 = times(back2_pair, b_hidden[...]) * slope(y1, t1)
        sent = rolled(back1, 1 if upward else -1) if axis == 2 else back1
        if (axis, upward) == PAIRS[0]:
            to_toward[...] = back1.reshape(shape)
            to_source[...] = sent.reshape(shape)
        else:
            add_rows(to_toward, axis, upward, back1)
            add_rows(to_source, axis, not upward, sent)
    back_toward = to_toward[...].reshape(around.shape)
    toward_pair = split(back_toward)
    source_pair = split(to_source[...].reshape(around.shape))
    total = direct_ref[...] + times(toward_pair, b_toward[...]) + times(source_pair, b_source[...])
    feat_out[...] = pick_rows(one_hot(order[0]), total)
    grads[0:c] += across(pair, toward_pair)
    grads[c:2 * c] += across(pair, source_pair)
    grads[2 * c:3 * c] += across(left[...], right[...])
    grads[3 * c:4 * c] += across(split(summed_ref[...]), around_pair)
    grads[4 * c:4 * c + 1] += column_sum(back_toward)
    grads[4 * c + 1:4 * c + 2] += back2_sum
    grads[4 * c + 2:4 * c + 3] += column_sum(around * degree(*around.shape))


def slot_at(place, at):
    slot = jnp.int32(0)
    for s in range(ELEM_DEV):
        slot = slot + jnp.where(place[0, s] == at, jnp.int32(s), jnp.int32(0))
    return slot


def on_elements(kernel, place, arrays, slotted, weights, order, out_rows, out_slotted, grads, scratch, cost):
    channels = arrays[0].shape[1]
    by_slot = pl.BlockSpec((NODES_EL, channels), lambda p, place: (slot_at(place, p), 0))
    by_place = pl.BlockSpec((NODES_EL, channels), lambda p, place: (p, 0))

    def whole(array):
        zeros = (0,) * array.ndim
        return pl.BlockSpec(array.shape, lambda p, place: zeros)

    order3 = order.reshape(order.shape[0], 1, order.shape[1])
    in_specs = [by_slot if s else by_place for s in slotted]
    in_specs.append(pl.BlockSpec((1, 1, order.shape[1]), lambda p, place: (slot_at(place, p), 0, 0)))
    in_specs += [whole(w) for w in weights]
    rows = order.shape[0] * NODES_EL
    out_shape = [jax.ShapeDtypeStruct((rows, channels), F32) for _ in range(out_rows)]
    out_specs = [by_slot if s else by_place for s in out_slotted]
    if grads:
        total = jax.ShapeDtypeStruct((4 * channels + SIDE, channels), F32)
        out_shape.append(total)
        out_specs.append(whole(total))
    return pl.pallas_call(
        kernel,
        grid_spec=pltpu.PrefetchScalarGridSpec(
            num_scalar_prefetch=1,
            grid=(order.shape[0],),
            in_specs=in_specs,
            out_specs=out_specs,
            scratch_shapes=scratch,
        ),
        out_shape=out_shape,
        cost_estimate=cost,
        compiler_params=pltpu.CompilerParams(
            dimension_semantics=("arbitrary",), vmem_limit_bytes=VMEM_BYTES
        ),
    )(place, *arrays, order3, *weights)


def plane(axis, element, side):
    base = element * NODES_EL
    far = (SIDE - 1) * side
    if axis == 0:
        return [(pl.ds(base + far * SIDE * SIDE, SIDE * SIDE), SIDE * SIDE)]
    if axis == 1:
        return [(pl.ds(base + x * SIDE * SIDE + far * SIDE, SIDE), SIDE) for x in range(SIDE)]
    return [(pl.ds(base + far, SIDE * SIDE, stride=SIDE), SIDE * SIDE)]


def exchange_kernel(devices, field_in, field, outgoing, arriving, send_sem, recv_sem):
    me = lax.axis_index("dom")
    depth = devices // (DGX * DGY)
    grid = (me % DGX, me // DGX % DGY, me // (DGX * DGY))
    limits = (DGX, DGY, depth)
    strides = (1, DGX, DGX * DGY)
    exists = []
    partner = []
    for axis in range(3):
        exists.append((grid[axis] > 0, grid[axis] < limits[axis] - 1))
        partner.append(
            (
                jnp.where(exists[axis][0], me - strides[axis], me + strides[axis]),
                jnp.where(exists[axis][1], me + strides[axis], me - strides[axis]),
            )
        )
    barrier = pltpu.get_barrier_semaphore()
    for axis in range(3):
        for side in range(2):

            @pl.when(exists[axis][side])
            def _():
                pl.semaphore_signal(
                    barrier, inc=1, device_id=(partner[axis][side],), device_id_type=pl.DeviceIdType.MESH
                )

    field[...] = field_in[...]
    peers = jnp.int32(0)
    for axis in range(3):
        for side in range(2):
            peers = peers + jnp.where(exists[axis][side], jnp.int32(1), jnp.int32(0))
    pl.semaphore_wait(barrier, peers)
    for axis in (2, 1, 0):
        weight = (4, 2, 1)[axis]
        sides = [[p for p in range(ELEM_DEV) if p // weight % 2 == side] for side in range(2)]
        copies = []
        for side in range(2):
            at = 0
            for element in sides[side]:
                for rows, count in plane(axis, element, side):
                    outgoing[axis, side, at:at + count] = field[rows]
                    at += count
            copies.append(
                pltpu.make_async_remote_copy(
                    src_ref=outgoing.at[axis, side],
                    dst_ref=arriving.at[axis, 1 - side],
                    send_sem=send_sem.at[axis, side],
                    recv_sem=recv_sem.at[axis, 1 - side],
                    device_id=(partner[axis][side],),
                    device_id_type=pl.DeviceIdType.MESH,
                )
            )
        for side in range(2):

            @pl.when(exists[axis][side])
            def _():
                copies[side].start()

        for lower, upper in zip(*sides):
            for (rows_l, _), (rows_u, _) in zip(plane(axis, lower, 1), plane(axis, upper, 0)):
                both = field[rows_l] + field[rows_u]
                field[rows_l] = both
                field[rows_u] = both
        for side in range(2):

            @pl.when(exists[axis][side])
            def _():
                copies[1 - side].wait_recv()
                at = 0
                for element in sides[side]:
                    for rows, count in plane(axis, element, side):
                        field[rows] += arriving[axis, side, at:at + count]
                        at += count
                copies[side].wait_send()


def make_consistent(field, collective):
    devices = lax.axis_size("dom")
    face = ELEM_DEV // 2 * SIDE * SIDE
    channels = field.shape[1]
    return pl.pallas_call(
        functools.partial(exchange_kernel, devices),
        out_shape=jax.ShapeDtypeStruct(field.shape, F32),
        in_specs=[pl.BlockSpec(memory_space=pltpu.VMEM)],
        out_specs=pl.BlockSpec(memory_space=pltpu.VMEM),
        scratch_shapes=[
            pltpu.VMEM((3, 2, face, channels), F32),
            pltpu.VMEM((3, 2, face, channels), F32),
            pltpu.SemaphoreType.DMA((3, 2)),
            pltpu.SemaphoreType.DMA((3, 2)),
        ],
        compiler_params=pltpu.CompilerParams(
            collective_id=collective, has_side_effects=True, vmem_limit_bytes=VMEM_BYTES
        ),
    )(field)


def total_kernel(devices, scale, edge, node, *refs):
    outs, (work, result, arriving, send_sem, recv_sem) = refs[:6], refs[6:]
    me = lax.axis_index("dom")
    bits = devices.bit_length() - 1
    side = [me // 2**k % 2 for k in range(bits)]
    partner = [me + 2**k - 2 * 2**k * side[k] for k in range(bits)]
    barrier = pltpu.get_barrier_semaphore()
    for k in range(bits):
        pl.semaphore_signal(barrier, inc=1, device_id=(partner[k],), device_id_type=pl.DeviceIdType.MESH)
    each = edge.shape[0]
    rows = work.shape[0]
    work[0:each] = edge[...]
    work[each:2 * each] = node[...]
    if rows > 2 * each:
        work[2 * each:rows] = jnp.zeros((rows - 2 * each, work.shape[1]), F32)
    pl.semaphore_wait(barrier, bits)

    def send(source, target, step, to):
        return pltpu.make_async_remote_copy(
            src_ref=source,
            dst_ref=target,
            send_sem=send_sem.at[step],
            recv_sem=recv_sem.at[step],
            device_id=(to,),
            device_id_type=pl.DeviceIdType.MESH,
        )

    start = jnp.int32(0)
    offset = 0
    size = rows
    starts = []
    for k in range(bits):
        size //= 2
        keep = pl.multiple_of(start + side[k] * size, SIDE)
        give = pl.multiple_of(start + (1 - side[k]) * size, SIDE)
        landing = arriving.at[pl.ds(offset, size)]
        copy = send(work.at[pl.ds(give, size)], landing, k, partner[k])
        copy.start()
        copy.wait()
        work[pl.ds(keep, size)] += arriving[offset:offset + size]
        offset += size
        start = keep
        starts.append(keep)
    result[pl.ds(start, size)] = work[pl.ds(start, size)] * scale
    for k in reversed(range(bits)):
        block = result.at[pl.ds(starts[k], size)]
        copy = send(block, block, bits + k, partner[k])
        copy.start()
        copy.wait()
        size *= 2
    for base, (first, middle, bias) in ((0, outs[:3]), (each, outs[3:])):
        c = result.shape[1]
        first[...] = result[base:base + 2 * c]
        middle[...] = result[base + 2 * c:base + 4 * c]
        bias[...] = result[base + 4 * c:base + 4 * c + 3]


def sum_over_devices(edge, node, scale, collective):
    devices = lax.axis_size("dom")
    channels = edge.shape[1]
    unit = SIDE * devices
    rows = -(-2 * edge.shape[0] // unit) * unit
    group = [jax.ShapeDtypeStruct((n, channels), F32) for n in (2 * channels, 2 * channels, 3)]
    steps = 2 * (devices.bit_length() - 1)
    in_vmem = pl.BlockSpec(memory_space=pltpu.VMEM)
    outs = pl.pallas_call(
        functools.partial(total_kernel, devices, scale),
        out_shape=group + group,
        in_specs=[in_vmem] * 2,
        out_specs=[in_vmem] * 6,
        scratch_shapes=[pltpu.VMEM((rows, channels), F32)] * 3
        + [pltpu.SemaphoreType.DMA((steps,))] * 2,
        compiler_params=pltpu.CompilerParams(
            collective_id=collective, has_side_effects=True, vmem_limit_bytes=VMEM_BYTES
        ),
    )(edge, node)
    middle = (2, channels, channels)
    return (
        outs[0], outs[1].reshape(middle), outs[2],
        outs[3], outs[4].reshape(middle), outs[5],
    )


def body(
    node_feat,
    out_grad,
    lattice_of,
    element_place,
    edge_in,
    edge_mid,
    edge_bias,
    node_in,
    node_mid,
    node_bias,
):
    channels = node_feat.shape[1]
    cube = pltpu.VMEM((SIDE, SIDE, SIDE, channels), F32)
    wide = pltpu.VMEM((2 * channels, 2 * channels), BF16)
    pairs = 4 * (NODES_EL - SIDE * SIDE) + 2 * NODES_EL
    edge = (edge_in, edge_mid, edge_bias)
    node = (node_in, node_mid, node_bias)

    def cost(rows):
        return pl.CostEstimate(
            flops=8 * rows * channels * channels * lattice_of.shape[0],
            bytes_accessed=16 * node_feat.size,
            transcendentals=0,
        )

    lattice, summed, local = on_elements(
        edge_forward_kernel, element_place, [node_feat], [True], edge, lattice_of,
        3, [False] * 3, False, [cube] * 3 + [wide] * 4, cost(pairs),
    )
    gathered = make_consistent(local, 0)
    new_feat, direct, around, node_total = on_elements(
        node_kernel, element_place, [lattice, gathered, out_grad], [False, False, True], node, lattice_of,
        3, [True, False, False], True, [wide] * 8, cost(12 * NODES_EL),
    )
    around = make_consistent(around, 1)
    tall = pltpu.VMEM((pairs, 2 * channels), BF16)
    feat_grad, edge_total = on_elements(
        edge_backward_kernel, element_place, [lattice, around, summed, direct], [False] * 4, edge, lattice_of,
        1, [True], True, [cube] * 5 + [tall] * 2 + [wide] * 7, cost(3 * pairs),
    )
    scale = 1.0 / math.sqrt(lax.axis_size("dom") * ELEM_DEV * NODES_EL)
    return (new_feat, feat_grad) + sum_over_devices(edge_total, node_total, scale, 2)


def solution(mesh):
    in_specs = (
        P("dom", None),
        P("dom", None),
        P("dom", None),
        P("dom", None),
        P(),
        P(),
        P(),
        P(),
        P(),
        P(),
    )
    out_specs = (P("dom", None), P("dom", None), P(), P(), P(), P(), P(), P())
    return jax.shard_map(body, mesh=mesh, in_specs=in_specs, out_specs=out_specs, check_vma=False)
```

```python
import functools
import math

import jax
import jax.numpy as jnp
from jax import lax
from jax.experimental import pallas as pl
from jax.experimental.pallas import tpu as pltpu
from jax.sharding import PartitionSpec as P

SIDE = 8
ELEM_DEV = 8
DGX = 4
DGY = 4
NODES_EL = 512

F32 = jnp.float32
BF16 = jnp.bfloat16
VMEM_BYTES = 20 * 2**20
PAIRS = ((2, True), (2, False), (0, True), (0, False), (1, True), (1, False))


def split(values):
    high = values.astype(BF16)
    low = (values - high.astype(F32)).astype(BF16)
    return jnp.concatenate([high, low], axis=1)


def spread(weight):
    halves = split(weight)
    return jnp.concatenate([halves, halves], axis=0)


def times(pair, spread_weight):
    wide = jnp.dot(pair, spread_weight, preferred_element_type=F32)
    half = wide.shape[1] // 2
    return wide[:, :half] + wide[:, half:]


def across(left, right):
    wide = lax.dot_general(left, right, (((0,), (0,)), ((), ())), preferred_element_type=F32)
    m, n = wide.shape[0] // 2, wide.shape[1] // 2
    return (wide[:m, :n] + wide[m:, n:]) + (wide[:m, n:] + wide[m:, :n])


def column_sum(values):
    return jnp.sum(values, axis=0, keepdims=True)


def one_hot(order):
    n = order.shape[1]
    points = lax.broadcasted_iota(jnp.int32, (n, n), 0)
    return jnp.where(points == order, 1.0, 0.0).astype(BF16)


def place_rows(hot, values):
    wide = jnp.dot(hot, split(values), preferred_element_type=F32)
    half = wide.shape[1] // 2
    return wide[:, :half] + wide[:, half:]


def pick_rows(hot, values):
    wide = lax.dot_general(hot, split(values), (((0,), (0,)), ((), ())), preferred_element_type=F32)
    half = wide.shape[1] // 2
    return wide[:, :half] + wide[:, half:]


def slope(half_value, tanh):
    return (1.0 + tanh) * (1.0 + half_value * (1.0 - tanh))


def window(axis, first):
    index = [slice(None)] * 3
    if axis != 2:
        index[axis] = slice(0, SIDE - 1) if first else slice(1, SIDE)
    return tuple(index)


def rows_of(ref, axis, first):
    picked = ref[window(axis, first)]
    return picked.reshape(-1, picked.shape[-1])


def rolled(rows, shift):
    grouped = rows.reshape(-1, SIDE, rows.shape[-1])
    return pltpu.roll(grouped, shift % SIDE, 1).reshape(rows.shape)


def add_rows(ref, axis, first, rows):
    index = window(axis, first)
    ref[index] += rows.reshape(ref[index].shape)


def inner(rows, channels, upward):
    z = lax.broadcasted_iota(jnp.int32, (rows, channels), 0) % SIDE
    return z < SIDE - 1 if upward else z > 0


def degree(rows, channels):
    at = lax.broadcasted_iota(jnp.int32, (rows, channels), 0)
    total = jnp.zeros((rows, channels), F32)
    for coordinate in (at // (SIDE * SIDE), at // SIDE % SIDE, at % SIDE):
        edge = (coordinate == 0) | (coordinate == SIDE - 1)
        total = total + jnp.where(edge, 1.0, 2.0)
    return total


def senders(source, axis, upward):
    if axis == 2:
        whole = source[...].reshape(-1, source.shape[-1])
        return rolled(whole, -1 if upward else 1)
    return rows_of(source, axis, not upward)


def edge_forward_kernel(
    place, feat, order, w_in, w_mid, bias,
    lattice_out, summed_out, local_out,
    toward, source, total, w_toward, w_source, w_hidden, w_last,
):
    channels = feat.shape[1]

    @pl.when(pl.program_id(0) == 0)
    def _():
        w_toward[...] = spread(0.5 * w_in[:channels])
        w_source[...] = spread(0.5 * w_in[channels:])
        w_hidden[...] = spread(0.5 * w_mid[0])
        w_last[...] = spread(w_mid[1])

    lattice = place_rows(one_hot(order[0]), feat[...])
    lattice_out[...] = lattice
    pair = split(lattice)
    shape = toward.shape
    toward[...] = (times(pair, w_toward[...]) + 0.5 * bias[0:1]).reshape(shape)
    source[...] = times(pair, w_source[...]).reshape(shape)
    bias_half = 0.5 * bias[1:2]
    for axis, upward in PAIRS:
        y = rows_of(toward, axis, upward) + senders(source, axis, upward)
        hidden = y + y * jnp.tanh(y)
        y = times(split(hidden), w_hidden[...]) + bias_half
        hidden = y + y * jnp.tanh(y)
        if axis == 2:
            hidden = jnp.where(inner(*hidden.shape, upward), hidden, 0.0)
        if (axis, upward) == PAIRS[0]:
            total[...] = hidden.reshape(shape)
        else:
            add_rows(total, axis, upward, hidden)
    summed = total[...].reshape(lattice.shape)
    summed_out[...] = summed
    local_out[...] = times(split(summed), w_last[...]) + degree(*lattice.shape) * bias[2:3]


def node_kernel(
    place, lattice_ref, gathered_ref, cotangent, order, w_in, w_mid, bias,
    new_out, direct_out, around_out, grads,
    w_own, w_near, w_hidden, w_last, b_own, b_near, b_hidden, b_last,
):
    channels = lattice_ref.shape[1]

    @pl.when(pl.program_id(0) == 0)
    def _():
        w_own[...] = spread(0.5 * w_in[:channels])
        w_near[...] = spread(0.5 * w_in[channels:])
        w_hidden[...] = spread(0.5 * w_mid[0])
        w_last[...] = spread(w_mid[1])
        b_own[...] = spread(w_in[:channels].T)
        b_near[...] = spread(w_in[channels:].T)
        b_hidden[...] = spread(0.5 * w_mid[0].T)
        b_last[...] = spread(0.5 * w_mid[1].T)
        grads[...] = jnp.zeros(grads.shape, F32)

    hot = one_hot(order[0])
    lattice = lattice_ref[...]
    own = split(lattice)
    near = split(gathered_ref[...])
    y1 = times(own, w_own[...]) + times(near, w_near[...]) + 0.5 * bias[0:1]
    t1 = jnp.tanh(y1)
    hidden1 = split(y1 + y1 * t1)
    y2 = times(hidden1, w_hidden[...]) + 0.5 * bias[1:2]
    t2 = jnp.tanh(y2)
    hidden2 = split(y2 + y2 * t2)
    new_out[...] = pick_rows(hot, lattice + times(hidden2, w_last[...]) + bias[2:3])

    incoming = place_rows(hot, cotangent[...])
    incoming_pair = split(incoming)
    back2 = times(incoming_pair, b_last[...]) * slope(y2, t2)
    back2_pair = split(back2)
    back1 = times(back2_pair, b_hidden[...]) * slope(y1, t1)
    back1_pair = split(back1)
    direct_out[...] = incoming + times(back1_pair, b_own[...])
    around_out[...] = times(back1_pair, b_near[...])
    c = channels
    grads[0:c] += across(own, back1_pair)
    grads[c:2 * c] += across(near, back1_pair)
    grads[2 * c:3 * c] += across(hidden1, back2_pair)
    grads[3 * c:4 * c] += across(hidden2, incoming_pair)
    grads[4 * c:4 * c + 1] += column_sum(back1)
    grads[4 * c + 1:4 * c + 2] += column_sum(back2)
    grads[4 * c + 2:4 * c + 3] += column_sum(incoming)


def edge_backward_kernel(
    place, lattice_ref, around_ref, summed_ref, direct_ref, order, w_in, w_mid, bias,
    feat_out, grads,
    toward, source, incoming, to_toward, to_source, left, right,
    w_toward, w_source, w_hidden, b_toward, b_source, b_hidden, b_last,
):
    channels = lattice_ref.shape[1]
    c = channels

    @pl.when(pl.program_id(0) == 0)
    def _():
        w_toward[...] = spread(0.5 * w_in[:channels])
        w_source[...] = spread(0.5 * w_in[channels:])
        w_hidden[...] = spread(0.5 * w_mid[0])
        b_toward[...] = spread(w_in[:channels].T)
        b_source[...] = spread(w_in[channels:].T)
        b_hidden[...] = spread(0.5 * w_mid[0].T)
        b_last[...] = spread(0.5 * w_mid[1].T)
        grads[...] = jnp.zeros(grads.shape, F32)

    around = around_ref[...]
    around_pair = split(around)
    shape = toward.shape
    pair = split(lattice_ref[...])
    toward[...] = (times(pair, w_toward[...]) + 0.5 * bias[0:1]).reshape(shape)
    source[...] = times(pair, w_source[...]).reshape(shape)
    incoming[...] = times(around_pair, b_last[...]).reshape(shape)
    bias_half = 0.5 * bias[1:2]
    back2_sum = jnp.zeros((1, channels), F32)
    start = 0
    for axis, upward in PAIRS:
        y1 = rows_of(toward, axis, upward) + senders(source, axis, upward)
        rows = y1.shape[0]
        span = slice(start, start + rows)
        start += rows
        t1 = jnp.tanh(y1)
        hidden_pair = split(y1 + y1 * t1)
        left[span] = hidden_pair
        y2 = times(hidden_pair, w_hidden[...]) + bias_half
        t2 = jnp.tanh(y2)
        arrived = rows_of(incoming, axis, upward)
        if axis == 2:
            arrived = jnp.where(inner(*arrived.shape, upward), arrived, 0.0)
        back2 = arrived * slope(y2, t2)
        back2_sum = back2_sum + column_sum(back2)
        back2_pair = split(back2)
        right[span] = back2_pair
        back1 = times(back2_pair, b_hidden[...]) * slope(y1, t1)
        sent = rolled(back1, 1 if upward else -1) if axis == 2 else back1
        if (axis, upward) == PAIRS[0]:
            to_toward[...] = back1.reshape(shape)
            to_source[...] = sent.reshape(shape)
        else:
            add_rows(to_toward, axis, upward, back1)
            add_rows(to_source, axis, not upward, sent)
    back_toward = to_toward[...].reshape(around.shape)
    toward_pair = split(back_toward)
    source_pair = split(to_source[...].reshape(around.shape))
    total = direct_ref[...] + times(toward_pair, b_toward[...]) + times(source_pair, b_source[...])
    feat_out[...] = pick_rows(one_hot(order[0]), total)
    grads[0:c] += across(pair, toward_pair)
    grads[c:2 * c] += across(pair, source_pair)
    grads[2 * c:3 * c] += across(left[...], right[...])
    grads[3 * c:4 * c] += across(split(summed_ref[...]), around_pair)
    grads[4 * c:4 * c + 1] += column_sum(back_toward)
    grads[4 * c + 1:4 * c + 2] += back2_sum
    grads[4 * c + 2:4 * c + 3] += column_sum(around * degree(*around.shape))


def slot_at(place, at):
    slot = jnp.int32(0)
    for s in range(ELEM_DEV):
        slot = slot + jnp.where(place[0, s] == at, jnp.int32(s), jnp.int32(0))
    return slot


def on_elements(kernel, place, arrays, slotted, weights, order, out_rows, out_slotted, grads, scratch, cost):
    channels = arrays[0].shape[1]
    by_slot = pl.BlockSpec((NODES_EL, channels), lambda p, place: (slot_at(place, p), 0))
    by_place = pl.BlockSpec((NODES_EL, channels), lambda p, place: (p, 0))

    def whole(array):
        zeros = (0,) * array.ndim
        return pl.BlockSpec(array.shape, lambda p, place: zeros)

    order3 = order.reshape(order.shape[0], 1, order.shape[1])
    in_specs = [by_slot if s else by_place for s in slotted]
    in_specs.append(pl.BlockSpec((1, 1, order.shape[1]), lambda p, place: (slot_at(place, p), 0, 0)))
    in_specs += [whole(w) for w in weights]
    rows = order.shape[0] * NODES_EL
    out_shape = [jax.ShapeDtypeStruct((rows, channels), F32) for _ in range(out_rows)]
    out_specs = [by_slot if s else by_place for s in out_slotted]
    if grads:
        total = jax.ShapeDtypeStruct((4 * channels + SIDE, channels), F32)
        out_shape.append(total)
        out_specs.append(whole(total))
    return pl.pallas_call(
        kernel,
        grid_spec=pltpu.PrefetchScalarGridSpec(
            num_scalar_prefetch=1,
            grid=(order.shape[0],),
            in_specs=in_specs,
            out_specs=out_specs,
            scratch_shapes=scratch,
        ),
        out_shape=out_shape,
        cost_estimate=cost,
        compiler_params=pltpu.CompilerParams(
            dimension_semantics=("arbitrary",), vmem_limit_bytes=VMEM_BYTES
        ),
    )(place, *arrays, order3, *weights)


def plane(axis, element, side):
    base = element * NODES_EL
    far = (SIDE - 1) * side
    if axis == 0:
        return [(pl.ds(base + far * SIDE * SIDE, SIDE * SIDE), SIDE * SIDE)]
    if axis == 1:
        return [(pl.ds(base + x * SIDE * SIDE + far * SIDE, SIDE), SIDE) for x in range(SIDE)]
    return [(pl.ds(base + far, SIDE * SIDE, stride=SIDE), SIDE * SIDE)]


def exchange_kernel(devices, field_in, field, outgoing, arriving, send_sem, recv_sem):
    me = lax.axis_index("dom")
    depth = devices // (DGX * DGY)
    grid = (me % DGX, me // DGX % DGY, me // (DGX * DGY))
    limits = (DGX, DGY, depth)
    strides = (1, DGX, DGX * DGY)
    exists = []
    partner = []
    for axis in range(3):
        exists.append((grid[axis] > 0, grid[axis] < limits[axis] - 1))
        partner.append(
            (
                jnp.where(exists[axis][0], me - strides[axis], me + strides[axis]),
                jnp.where(exists[axis][1], me + strides[axis], me - strides[axis]),
            )
        )
    barrier = pltpu.get_barrier_semaphore()
    for axis in range(3):
        for side in range(2):

            @pl.when(exists[axis][side])
            def _():
                pl.semaphore_signal(
                    barrier, inc=1, device_id=(partner[axis][side],), device_id_type=pl.DeviceIdType.MESH
                )

    field[...] = field_in[...]
    peers = jnp.int32(0)
    for axis in range(3):
        for side in range(2):
            peers = peers + jnp.where(exists[axis][side], jnp.int32(1), jnp.int32(0))
    pl.semaphore_wait(barrier, peers)
    for axis in (2, 1, 0):
        weight = (4, 2, 1)[axis]
        sides = [[p for p in range(ELEM_DEV) if p // weight % 2 == side] for side in range(2)]
        copies = []
        for side in range(2):
            at = 0
            for element in sides[side]:
                for rows, count in plane(axis, element, side):
                    outgoing[axis, side, at:at + count] = field[rows]
                    at += count
            copies.append(
                pltpu.make_async_remote_copy(
                    src_ref=outgoing.at[axis, side],
                    dst_ref=arriving.at[axis, 1 - side],
                    send_sem=send_sem.at[axis, side],
                    recv_sem=recv_sem.at[axis, 1 - side],
                    device_id=(partner[axis][side],),
                    device_id_type=pl.DeviceIdType.MESH,
                )
            )
        for side in range(2):

            @pl.when(exists[axis][side])
            def _():
                copies[side].start()

        for lower, upper in zip(*sides):
            for (rows_l, _), (rows_u, _) in zip(plane(axis, lower, 1), plane(axis, upper, 0)):
                both = field[rows_l] + field[rows_u]
                field[rows_l] = both
                field[rows_u] = both
        for side in range(2):

            @pl.when(exists[axis][side])
            def _():
                copies[1 - side].wait_recv()
                at = 0
                for element in sides[side]:
                    for rows, count in plane(axis, element, side):
                        field[rows] += arriving[axis, side, at:at + count]
                        at += count
                copies[side].wait_send()


def make_consistent(field, collective):
    devices = lax.axis_size("dom")
    face = ELEM_DEV // 2 * SIDE * SIDE
    channels = field.shape[1]
    return pl.pallas_call(
        functools.partial(exchange_kernel, devices),
        out_shape=jax.ShapeDtypeStruct(field.shape, F32),
        in_specs=[pl.BlockSpec(memory_space=pltpu.VMEM)],
        out_specs=pl.BlockSpec(memory_space=pltpu.VMEM),
        scratch_shapes=[
            pltpu.VMEM((3, 2, face, channels), F32),
            pltpu.VMEM((3, 2, face, channels), F32),
            pltpu.SemaphoreType.DMA((3, 2)),
            pltpu.SemaphoreType.DMA((3, 2)),
        ],
        compiler_params=pltpu.CompilerParams(
            collective_id=collective, has_side_effects=True, vmem_limit_bytes=VMEM_BYTES
        ),
    )(field)


def digits(devices):
    found = []
    low = 1
    while low < devices:
        radix = 2 if low == 1 or devices // low % 4 else 4
        found.append((low, radix))
        low *= radix
    return found


def total_kernel(devices, scale, edge, node, *refs):
    outs, (work, result, arriving, send_sem, recv_sem) = refs[:6], refs[6:]
    me = lax.axis_index("dom")
    stages = digits(devices)
    peers = [
        [(me // low % radix + j) % radix for j in range(radix)] for low, radix in stages
    ]
    barrier = pltpu.get_barrier_semaphore()
    for (low, radix), digit in zip(stages, peers):
        for j in range(1, radix):
            to = me + (digit[j] - digit[0]) * low
            pl.semaphore_signal(barrier, inc=1, device_id=(to,), device_id_type=pl.DeviceIdType.MESH)
    each = edge.shape[0]
    rows = work.shape[0]
    work[0:each] = edge[...]
    work[each:2 * each] = node[...]
    if rows > 2 * each:
        work[2 * each:rows] = jnp.zeros((rows - 2 * each, work.shape[1]), F32)
    pl.semaphore_wait(barrier, sum(radix - 1 for _, radix in stages))

    def send(source, target, step, to):
        return pltpu.make_async_remote_copy(
            src_ref=source,
            dst_ref=target,
            send_sem=send_sem.at[step],
            recv_sem=recv_sem.at[step],
            device_id=(to,),
            device_id_type=pl.DeviceIdType.MESH,
        )

    start = jnp.int32(0)
    offset = 0
    size = rows
    step = 0
    starts = []
    for (low, radix), digit in zip(stages, peers):
        size //= radix
        copies = []
        landings = []
        for j in range(1, radix):
            give = pl.multiple_of(start + digit[j] * size, SIDE)
            to = me + (digit[j] - digit[0]) * low
            copy = send(work.at[pl.ds(give, size)], arriving.at[pl.ds(offset, size)], step, to)
            copy.start()
            copies.append(copy)
            landings.append(offset)
            offset += size
            step += 1
        starts.append(start)
        start = pl.multiple_of(start + digit[0] * size, SIDE)
        for copy, landing in zip(copies, landings):
            copy.wait()
            work[pl.ds(start, size)] += arriving[landing:landing + size]
    result[pl.ds(start, size)] = work[pl.ds(start, size)] * scale
    for (low, radix), digit, before in reversed(list(zip(stages, peers, starts))):
        block = result.at[pl.ds(start, size)]
        copies = []
        for j in range(1, radix):
            to = me + (digit[j] - digit[0]) * low
            copy = send(block, block, step, to)
            copy.start()
            copies.append(copy)
            step += 1
        for copy in copies:
            copy.wait()
        start = before if isinstance(before, int) else pl.multiple_of(before, SIDE)
        size *= radix
    for base, (first, middle, bias) in ((0, outs[:3]), (each, outs[3:])):
        c = result.shape[1]
        first[...] = result[base:base + 2 * c]
        middle[...] = result[base + 2 * c:base + 4 * c]
        bias[...] = result[base + 4 * c:base + 4 * c + 3]


def sum_over_devices(edge, node, scale, collective):
    devices = lax.axis_size("dom")
    channels = edge.shape[1]
    unit = SIDE * devices
    rows = -(-2 * edge.shape[0] // unit) * unit
    group = [jax.ShapeDtypeStruct((n, channels), F32) for n in (2 * channels, 2 * channels, 3)]
    steps = 2 * sum(radix - 1 for _, radix in digits(devices))
    in_vmem = pl.BlockSpec(memory_space=pltpu.VMEM)
    outs = pl.pallas_call(
        functools.partial(total_kernel, devices, scale),
        out_shape=group + group,
        in_specs=[in_vmem] * 2,
        out_specs=[in_vmem] * 6,
        scratch_shapes=[pltpu.VMEM((rows, channels), F32)] * 3
        + [pltpu.SemaphoreType.DMA((steps,))] * 2,
        compiler_params=pltpu.CompilerParams(
            collective_id=collective, has_side_effects=True, vmem_limit_bytes=VMEM_BYTES
        ),
    )(edge, node)
    middle = (2, channels, channels)
    return (
        outs[0], outs[1].reshape(middle), outs[2],
        outs[3], outs[4].reshape(middle), outs[5],
    )


def body(
    node_feat,
    out_grad,
    lattice_of,
    element_place,
    edge_in,
    edge_mid,
    edge_bias,
    node_in,
    node_mid,
    node_bias,
):
    channels = node_feat.shape[1]
    cube = pltpu.VMEM((SIDE, SIDE, SIDE, channels), F32)
    wide = pltpu.VMEM((2 * channels, 2 * channels), BF16)
    pairs = 4 * (NODES_EL - SIDE * SIDE) + 2 * NODES_EL
    edge = (edge_in, edge_mid, edge_bias)
    node = (node_in, node_mid, node_bias)

    def cost(rows):
        return pl.CostEstimate(
            flops=8 * rows * channels * channels * lattice_of.shape[0],
            bytes_accessed=16 * node_feat.size,
            transcendentals=0,
        )

    lattice, summed, local = on_elements(
        edge_forward_kernel, element_place, [node_feat], [True], edge, lattice_of,
        3, [False] * 3, False, [cube] * 3 + [wide] * 4, cost(pairs),
    )
    gathered = make_consistent(local, 0)
    new_feat, direct, around, node_total = on_elements(
        node_kernel, element_place, [lattice, gathered, out_grad], [False, False, True], node, lattice_of,
        3, [True, False, False], True, [wide] * 8, cost(12 * NODES_EL),
    )
    around = make_consistent(around, 1)
    tall = pltpu.VMEM((pairs, 2 * channels), BF16)
    feat_grad, edge_total = on_elements(
        edge_backward_kernel, element_place, [lattice, around, summed, direct], [False] * 4, edge, lattice_of,
        1, [True], True, [cube] * 5 + [tall] * 2 + [wide] * 7, cost(3 * pairs),
    )
    scale = 1.0 / math.sqrt(lax.axis_size("dom") * ELEM_DEV * NODES_EL)
    return (new_feat, feat_grad) + sum_over_devices(edge_total, node_total, scale, 2)


def solution(mesh):
    in_specs = (
        P("dom", None),
        P("dom", None),
        P("dom", None),
        P("dom", None),
        P(),
        P(),
        P(),
        P(),
        P(),
        P(),
    )
    out_specs = (P("dom", None), P("dom", None), P(), P(), P(), P(), P(), P())
    return jax.shard_map(body, mesh=mesh, in_specs=in_specs, out_specs=out_specs, check_vma=False)
```

```python
import functools
import math

import jax
import jax.numpy as jnp
from jax import lax
from jax.experimental import pallas as pl
from jax.experimental.pallas import tpu as pltpu
from jax.sharding import PartitionSpec as P

SIDE = 8
ELEM_DEV = 8
DGX = 4
DGY = 4
NODES_EL = 512

F32 = jnp.float32
BF16 = jnp.bfloat16
VMEM_BYTES = 20 * 2**20
PAIRS = ((2, True), (2, False), (0, True), (0, False), (1, True), (1, False))


def split(values):
    high = values.astype(BF16)
    low = (values - high.astype(F32)).astype(BF16)
    return jnp.concatenate([high, low], axis=1)


def spread(weight):
    halves = split(weight)
    return jnp.concatenate([halves, halves], axis=0)


def times(pair, spread_weight):
    wide = jnp.dot(pair, spread_weight, preferred_element_type=F32)
    half = wide.shape[1] // 2
    return wide[:, :half] + wide[:, half:]


def across(left, right):
    wide = lax.dot_general(left, right, (((0,), (0,)), ((), ())), preferred_element_type=F32)
    m, n = wide.shape[0] // 2, wide.shape[1] // 2
    return (wide[:m, :n] + wide[m:, n:]) + (wide[:m, n:] + wide[m:, :n])


def column_sum(values):
    return jnp.sum(values, axis=0, keepdims=True)


def one_hot(order):
    n = order.shape[1]
    points = lax.broadcasted_iota(jnp.int32, (n, n), 0)
    return jnp.where(points == order, 1.0, 0.0).astype(BF16)


def place_rows(hot, values):
    wide = jnp.dot(hot, split(values), preferred_element_type=F32)
    half = wide.shape[1] // 2
    return wide[:, :half] + wide[:, half:]


def pick_rows(hot, values):
    wide = lax.dot_general(hot, split(values), (((0,), (0,)), ((), ())), preferred_element_type=F32)
    half = wide.shape[1] // 2
    return wide[:, :half] + wide[:, half:]


def slope(half_value, tanh):
    return (1.0 + tanh) * (1.0 + half_value * (1.0 - tanh))


def window(axis, first):
    index = [slice(None)] * 3
    if axis != 2:
        index[axis] = slice(0, SIDE - 1) if first else slice(1, SIDE)
    return tuple(index)


def rows_of(ref, axis, first):
    picked = ref[window(axis, first)]
    return picked.reshape(-1, picked.shape[-1])


def rolled(rows, shift):
    grouped = rows.reshape(-1, SIDE, rows.shape[-1])
    return pltpu.roll(grouped, shift % SIDE, 1).reshape(rows.shape)


def add_rows(ref, axis, first, rows):
    index = window(axis, first)
    ref[index] += rows.reshape(ref[index].shape)


def inner(rows, channels, upward):
    z = lax.broadcasted_iota(jnp.int32, (rows, channels), 0) % SIDE
    return z < SIDE - 1 if upward else z > 0


def degree(rows, channels):
    at = lax.broadcasted_iota(jnp.int32, (rows, channels), 0)
    total = jnp.zeros((rows, channels), F32)
    for coordinate in (at // (SIDE * SIDE), at // SIDE % SIDE, at % SIDE):
        edge = (coordinate == 0) | (coordinate == SIDE - 1)
        total = total + jnp.where(edge, 1.0, 2.0)
    return total


def senders(source, axis, upward):
    if axis == 2:
        whole = source[...].reshape(-1, source.shape[-1])
        return rolled(whole, -1 if upward else 1)
    return rows_of(source, axis, not upward)


def edge_forward_kernel(
    place, feat, order, w_in, w_mid, bias,
    lattice_out, summed_out, local_out,
    toward, source, total, w_toward, w_source, w_hidden, w_last,
):
    channels = feat.shape[1]

    @pl.when(pl.program_id(0) == 0)
    def _():
        w_toward[...] = spread(0.5 * w_in[:channels])
        w_source[...] = spread(0.5 * w_in[channels:])
        w_hidden[...] = spread(0.5 * w_mid[0])
        w_last[...] = spread(w_mid[1])

    lattice = place_rows(one_hot(order[0]), feat[...])
    lattice_out[...] = lattice
    pair = split(lattice)
    shape = toward.shape
    toward[...] = (times(pair, w_toward[...]) + 0.5 * bias[0:1]).reshape(shape)
    source[...] = times(pair, w_source[...]).reshape(shape)
    bias_half = 0.5 * bias[1:2]
    for axis, upward in PAIRS:
        y = rows_of(toward, axis, upward) + senders(source, axis, upward)
        hidden = y + y * jnp.tanh(y)
        y = times(split(hidden), w_hidden[...]) + bias_half
        hidden = y + y * jnp.tanh(y)
        if axis == 2:
            hidden = jnp.where(inner(*hidden.shape, upward), hidden, 0.0)
        if (axis, upward) == PAIRS[0]:
            total[...] = hidden.reshape(shape)
        else:
            add_rows(total, axis, upward, hidden)
    summed = total[...].reshape(lattice.shape)
    summed_out[...] = summed
    local_out[...] = times(split(summed), w_last[...]) + degree(*lattice.shape) * bias[2:3]


def node_kernel(
    place, lattice_ref, gathered_ref, cotangent, order, w_in, w_mid, bias,
    new_out, direct_out, around_out, grads,
    w_own, w_near, w_hidden, w_last, b_own, b_near, b_hidden, b_last,
):
    channels = lattice_ref.shape[1]

    @pl.when(pl.program_id(0) == 0)
    def _():
        w_own[...] = spread(0.5 * w_in[:channels])
        w_near[...] = spread(0.5 * w_in[channels:])
        w_hidden[...] = spread(0.5 * w_mid[0])
        w_last[...] = spread(w_mid[1])
        b_own[...] = spread(w_in[:channels].T)
        b_near[...] = spread(w_in[channels:].T)
        b_hidden[...] = spread(0.5 * w_mid[0].T)
        b_last[...] = spread(0.5 * w_mid[1].T)
        grads[...] = jnp.zeros(grads.shape, F32)

    hot = one_hot(order[0])
    lattice = lattice_ref[...]
    own = split(lattice)
    near = split(gathered_ref[...])
    y1 = times(own, w_own[...]) + times(near, w_near[...]) + 0.5 * bias[0:1]
    t1 = jnp.tanh(y1)
    hidden1 = split(y1 + y1 * t1)
    y2 = times(hidden1, w_hidden[...]) + 0.5 * bias[1:2]
    t2 = jnp.tanh(y2)
    hidden2 = split(y2 + y2 * t2)
    new_out[...] = pick_rows(hot, lattice + times(hidden2, w_last[...]) + bias[2:3])

    incoming = place_rows(hot, cotangent[...])
    incoming_pair = split(incoming)
    back2 = times(incoming_pair, b_last[...]) * slope(y2, t2)
    back2_pair = split(back2)
    back1 = times(back2_pair, b_hidden[...]) * slope(y1, t1)
    back1_pair = split(back1)
    direct_out[...] = incoming + times(back1_pair, b_own[...])
    around_out[...] = times(back1_pair, b_near[...])
    c = channels
    grads[0:c] += across(own, back1_pair)
    grads[c:2 * c] += across(near, back1_pair)
    grads[2 * c:3 * c] += across(hidden1, back2_pair)
    grads[3 * c:4 * c] += across(hidden2, incoming_pair)
    grads[4 * c:4 * c + 1] += column_sum(back1)
    grads[4 * c + 1:4 * c + 2] += column_sum(back2)
    grads[4 * c + 2:4 * c + 3] += column_sum(incoming)


def edge_backward_kernel(
    place, lattice_ref, around_ref, summed_ref, direct_ref, order, w_in, w_mid, bias,
    feat_out, grads,
    toward, source, incoming, to_toward, to_source, left, right,
    w_toward, w_source, w_hidden, b_toward, b_source, b_hidden, b_last,
):
    channels = lattice_ref.shape[1]
    c = channels

    @pl.when(pl.program_id(0) == 0)
    def _():
        w_toward[...] = spread(0.5 * w_in[:channels])
        w_source[...] = spread(0.5 * w_in[channels:])
        w_hidden[...] = spread(0.5 * w_mid[0])
        b_toward[...] = spread(w_in[:channels].T)
        b_source[...] = spread(w_in[channels:].T)
        b_hidden[...] = spread(0.5 * w_mid[0].T)
        b_last[...] = spread(0.5 * w_mid[1].T)
        grads[...] = jnp.zeros(grads.shape, F32)

    around = around_ref[...]
    around_pair = split(around)
    shape = toward.shape
    pair = split(lattice_ref[...])
    toward[...] = (times(pair, w_toward[...]) + 0.5 * bias[0:1]).reshape(shape)
    source[...] = times(pair, w_source[...]).reshape(shape)
    incoming[...] = times(around_pair, b_last[...]).reshape(shape)
    bias_half = 0.5 * bias[1:2]
    back2_sum = jnp.zeros((1, channels), F32)
    start = 0
    for axis, upward in PAIRS:
        y1 = rows_of(toward, axis, upward) + senders(source, axis, upward)
        rows = y1.shape[0]
        span = slice(start, start + rows)
        start += rows
        t1 = jnp.tanh(y1)
        hidden_pair = split(y1 + y1 * t1)
        left[span] = hidden_pair
        y2 = times(hidden_pair, w_hidden[...]) + bias_half
        t2 = jnp.tanh(y2)
        arrived = rows_of(incoming, axis, upward)
        if axis == 2:
            arrived = jnp.where(inner(*arrived.shape, upward), arrived, 0.0)
        back2 = arrived * slope(y2, t2)
        back2_sum = back2_sum + column_sum(back2)
        back2_pair = split(back2)
        right[span] = back2_pair
        back1 = times(back2_pair, b_hidden[...]) * slope(y1, t1)
        sent = rolled(back1, 1 if upward else -1) if axis == 2 else back1
        if (axis, upward) == PAIRS[0]:
            to_toward[...] = back1.reshape(shape)
            to_source[...] = sent.reshape(shape)
        else:
            add_rows(to_toward, axis, upward, back1)
            add_rows(to_source, axis, not upward, sent)
    back_toward = to_toward[...].reshape(around.shape)
    toward_pair = split(back_toward)
    source_pair = split(to_source[...].reshape(around.shape))
    total = direct_ref[...] + times(toward_pair, b_toward[...]) + times(source_pair, b_source[...])
    feat_out[...] = pick_rows(one_hot(order[0]), total)
    grads[0:c] += across(pair, toward_pair)
    grads[c:2 * c] += across(pair, source_pair)
    grads[2 * c:3 * c] += across(left[...], right[...])
    grads[3 * c:4 * c] += across(split(summed_ref[...]), around_pair)
    grads[4 * c:4 * c + 1] += column_sum(back_toward)
    grads[4 * c + 1:4 * c + 2] += back2_sum
    grads[4 * c + 2:4 * c + 3] += column_sum(around * degree(*around.shape))


def slot_at(place, at):
    slot = jnp.int32(0)
    for s in range(ELEM_DEV):
        slot = slot + jnp.where(place[0, s] == at, jnp.int32(s), jnp.int32(0))
    return slot


def on_elements(kernel, place, arrays, slotted, weights, order, out_rows, out_slotted, grads, scratch, cost):
    channels = arrays[0].shape[1]
    by_slot = pl.BlockSpec((NODES_EL, channels), lambda p, place: (slot_at(place, p), 0))
    by_place = pl.BlockSpec((NODES_EL, channels), lambda p, place: (p, 0))

    def whole(array):
        zeros = (0,) * array.ndim
        return pl.BlockSpec(array.shape, lambda p, place: zeros)

    order3 = order.reshape(order.shape[0], 1, order.shape[1])
    in_specs = [by_slot if s else by_place for s in slotted]
    in_specs.append(pl.BlockSpec((1, 1, order.shape[1]), lambda p, place: (slot_at(place, p), 0, 0)))
    in_specs += [whole(w) for w in weights]
    rows = order.shape[0] * NODES_EL
    out_shape = [jax.ShapeDtypeStruct((rows, channels), F32) for _ in range(out_rows)]
    out_specs = [by_slot if s else by_place for s in out_slotted]
    if grads:
        total = jax.ShapeDtypeStruct((4 * channels + SIDE, channels), F32)
        out_shape.append(total)
        out_specs.append(whole(total))
    return pl.pallas_call(
        kernel,
        grid_spec=pltpu.PrefetchScalarGridSpec(
            num_scalar_prefetch=1,
            grid=(order.shape[0],),
            in_specs=in_specs,
            out_specs=out_specs,
            scratch_shapes=scratch,
        ),
        out_shape=out_shape,
        cost_estimate=cost,
        compiler_params=pltpu.CompilerParams(
            dimension_semantics=("arbitrary",), vmem_limit_bytes=VMEM_BYTES
        ),
    )(place, *arrays, order3, *weights)


def plane(axis, element, side):
    base = element * NODES_EL
    far = (SIDE - 1) * side
    if axis == 0:
        return [(pl.ds(base + far * SIDE * SIDE, SIDE * SIDE), SIDE * SIDE)]
    if axis == 1:
        return [(pl.ds(base + x * SIDE * SIDE + far * SIDE, SIDE), SIDE) for x in range(SIDE)]
    return [(pl.ds(base + far, SIDE * SIDE, stride=SIDE), SIDE * SIDE)]


def exchange_kernel(devices, field_in, field, outgoing, arriving, send_sem, recv_sem):
    me = lax.axis_index("dom")
    depth = devices // (DGX * DGY)
    grid = (me % DGX, me // DGX % DGY, me // (DGX * DGY))
    limits = (DGX, DGY, depth)
    strides = (1, DGX, DGX * DGY)
    exists = []
    partner = []
    for axis in range(3):
        exists.append((grid[axis] > 0, grid[axis] < limits[axis] - 1))
        partner.append(
            (
                jnp.where(exists[axis][0], me - strides[axis], me + strides[axis]),
                jnp.where(exists[axis][1], me + strides[axis], me - strides[axis]),
            )
        )
    barrier = pltpu.get_barrier_semaphore()
    for axis in range(3):
        for side in range(2):

            @pl.when(exists[axis][side])
            def _():
                pl.semaphore_signal(
                    barrier, inc=1, device_id=(partner[axis][side],), device_id_type=pl.DeviceIdType.MESH
                )

    field[...] = field_in[...]
    peers = jnp.int32(0)
    for axis in range(3):
        for side in range(2):
            peers = peers + jnp.where(exists[axis][side], jnp.int32(1), jnp.int32(0))
    pl.semaphore_wait(barrier, peers)
    def part(axis, side, half):
        weight = (4, 2, 1)[axis]
        return [p for p in range(ELEM_DEV) if p // weight % 2 == side and (axis == 0 or p // 4 == half)]

    def begin(axis, half):
        copies = []
        for side in range(2):
            first = at = half * outgoing.shape[2] // 2
            for element in part(axis, side, half):
                for rows, count in plane(axis, element, side):
                    outgoing[axis, side, at:at + count] = field[rows]
                    at += count
            span = pl.ds(first, at - first)
            copies.append(
                pltpu.make_async_remote_copy(
                    src_ref=outgoing.at[axis, side, span],
                    dst_ref=arriving.at[axis, 1 - side, span],
                    send_sem=send_sem.at[axis, side, half],
                    recv_sem=recv_sem.at[axis, 1 - side, half],
                    device_id=(partner[axis][side],),
                    device_id_type=pl.DeviceIdType.MESH,
                )
            )
        for side in range(2):

            @pl.when(exists[axis][side])
            def _():
                copies[side].start()

        for lower, upper in zip(part(axis, 0, half), part(axis, 1, half)):
            for (rows_l, _), (rows_u, _) in zip(plane(axis, lower, 1), plane(axis, upper, 0)):
                both = field[rows_l] + field[rows_u]
                field[rows_l] = both
                field[rows_u] = both
        return copies

    def finish(axis, half, copies):
        for side in range(2):

            @pl.when(exists[axis][side])
            def _():
                copies[1 - side].wait_recv()
                at = half * outgoing.shape[2] // 2
                for element in part(axis, side, half):
                    for rows, count in plane(axis, element, side):
                        field[rows] += arriving[axis, side, at:at + count]
                        at += count
                copies[side].wait_send()

    along_z = [begin(2, half) for half in range(2)]
    along_y = []
    for half in range(2):
        finish(2, half, along_z[half])
        along_y.append(begin(1, half))
    for half in range(2):
        finish(1, half, along_y[half])
    finish(0, 0, begin(0, 0))


def make_consistent(field, collective):
    devices = lax.axis_size("dom")
    face = ELEM_DEV // 2 * SIDE * SIDE
    channels = field.shape[1]
    return pl.pallas_call(
        functools.partial(exchange_kernel, devices),
        out_shape=jax.ShapeDtypeStruct(field.shape, F32),
        in_specs=[pl.BlockSpec(memory_space=pltpu.VMEM)],
        out_specs=pl.BlockSpec(memory_space=pltpu.VMEM),
        scratch_shapes=[
            pltpu.VMEM((3, 2, face, channels), F32),
            pltpu.VMEM((3, 2, face, channels), F32),
            pltpu.SemaphoreType.DMA((3, 2, 2)),
            pltpu.SemaphoreType.DMA((3, 2, 2)),
        ],
        compiler_params=pltpu.CompilerParams(
            collective_id=collective, has_side_effects=True, vmem_limit_bytes=VMEM_BYTES
        ),
    )(field)


def digits(devices):
    found = []
    low = 1
    while low < devices:
        radix = 2 if low == 1 or devices // low % 4 else 4
        found.append((low, radix))
        low *= radix
    return found


def total_kernel(devices, scale, edge, node, *refs):
    outs, (work, result, arriving, send_sem, recv_sem) = refs[:6], refs[6:]
    me = lax.axis_index("dom")
    stages = digits(devices)
    peers = [
        [(me // low % radix + j) % radix for j in range(radix)] for low, radix in stages
    ]
    barrier = pltpu.get_barrier_semaphore()
    for (low, radix), digit in zip(stages, peers):
        for j in range(1, radix):
            to = me + (digit[j] - digit[0]) * low
            pl.semaphore_signal(barrier, inc=1, device_id=(to,), device_id_type=pl.DeviceIdType.MESH)
    each = edge.shape[0]
    rows = work.shape[0]
    work[0:each] = edge[...]
    work[each:2 * each] = node[...]
    if rows > 2 * each:
        work[2 * each:rows] = jnp.zeros((rows - 2 * each, work.shape[1]), F32)
    pl.semaphore_wait(barrier, sum(radix - 1 for _, radix in stages))

    def send(source, target, step, to):
        return pltpu.make_async_remote_copy(
            src_ref=source,
            dst_ref=target,
            send_sem=send_sem.at[step],
            recv_sem=recv_sem.at[step],
            device_id=(to,),
            device_id_type=pl.DeviceIdType.MESH,
        )

    start = jnp.int32(0)
    offset = 0
    size = rows
    step = 0
    starts = []
    for (low, radix), digit in zip(stages, peers):
        size //= radix
        copies = []
        landings = []
        for j in range(1, radix):
            give = pl.multiple_of(start + digit[j] * size, SIDE)
            to = me + (digit[j] - digit[0]) * low
            copy = send(work.at[pl.ds(give, size)], arriving.at[pl.ds(offset, size)], step, to)
            copy.start()
            copies.append(copy)
            landings.append(offset)
            offset += size
            step += 1
        starts.append(start)
        start = pl.multiple_of(start + digit[0] * size, SIDE)
        for copy, landing in zip(copies, landings):
            copy.wait()
            work[pl.ds(start, size)] += arriving[landing:landing + size]
    result[pl.ds(start, size)] = work[pl.ds(start, size)] * scale
    for (low, radix), digit, before in reversed(list(zip(stages, peers, starts))):
        block = result.at[pl.ds(start, size)]
        copies = []
        for j in range(1, radix):
            to = me + (digit[j] - digit[0]) * low
            copy = send(block, block, step, to)
            copy.start()
            copies.append(copy)
            step += 1
        for copy in copies:
            copy.wait()
        start = before if isinstance(before, int) else pl.multiple_of(before, SIDE)
        size *= radix
    for base, (first, middle, bias) in ((0, outs[:3]), (each, outs[3:])):
        c = result.shape[1]
        first[...] = result[base:base + 2 * c]
        middle[...] = result[base + 2 * c:base + 4 * c]
        bias[...] = result[base + 4 * c:base + 4 * c + 3]


def sum_over_devices(edge, node, scale, collective):
    devices = lax.axis_size("dom")
    channels = edge.shape[1]
    unit = SIDE * devices
    rows = -(-2 * edge.shape[0] // unit) * unit
    group = [jax.ShapeDtypeStruct((n, channels), F32) for n in (2 * channels, 2 * channels, 3)]
    steps = 2 * sum(radix - 1 for _, radix in digits(devices))
    in_vmem = pl.BlockSpec(memory_space=pltpu.VMEM)
    outs = pl.pallas_call(
        functools.partial(total_kernel, devices, scale),
        out_shape=group + group,
        in_specs=[in_vmem] * 2,
        out_specs=[in_vmem] * 6,
        scratch_shapes=[pltpu.VMEM((rows, channels), F32)] * 3
        + [pltpu.SemaphoreType.DMA((steps,))] * 2,
        compiler_params=pltpu.CompilerParams(
            collective_id=collective, has_side_effects=True, vmem_limit_bytes=VMEM_BYTES
        ),
    )(edge, node)
    middle = (2, channels, channels)
    return (
        outs[0], outs[1].reshape(middle), outs[2],
        outs[3], outs[4].reshape(middle), outs[5],
    )


def body(
    node_feat,
    out_grad,
    lattice_of,
    element_place,
    edge_in,
    edge_mid,
    edge_bias,
    node_in,
    node_mid,
    node_bias,
):
    channels = node_feat.shape[1]
    cube = pltpu.VMEM((SIDE, SIDE, SIDE, channels), F32)
    wide = pltpu.VMEM((2 * channels, 2 * channels), BF16)
    pairs = 4 * (NODES_EL - SIDE * SIDE) + 2 * NODES_EL
    edge = (edge_in, edge_mid, edge_bias)
    node = (node_in, node_mid, node_bias)

    def cost(rows):
        return pl.CostEstimate(
            flops=8 * rows * channels * channels * lattice_of.shape[0],
            bytes_accessed=16 * node_feat.size,
            transcendentals=0,
        )

    lattice, summed, local = on_elements(
        edge_forward_kernel, element_place, [node_feat], [True], edge, lattice_of,
        3, [False] * 3, False, [cube] * 3 + [wide] * 4, cost(pairs),
    )
    gathered = make_consistent(local, 0)
    new_feat, direct, around, node_total = on_elements(
        node_kernel, element_place, [lattice, gathered, out_grad], [False, False, True], node, lattice_of,
        3, [True, False, False], True, [wide] * 8, cost(12 * NODES_EL),
    )
    around = make_consistent(around, 1)
    tall = pltpu.VMEM((pairs, 2 * channels), BF16)
    feat_grad, edge_total = on_elements(
        edge_backward_kernel, element_place, [lattice, around, summed, direct], [False] * 4, edge, lattice_of,
        1, [True], True, [cube] * 5 + [tall] * 2 + [wide] * 7, cost(3 * pairs),
    )
    scale = 1.0 / math.sqrt(lax.axis_size("dom") * ELEM_DEV * NODES_EL)
    return (new_feat, feat_grad) + sum_over_devices(edge_total, node_total, scale, 2)


def solution(mesh):
    in_specs = (
        P("dom", None),
        P("dom", None),
        P("dom", None),
        P("dom", None),
        P(),
        P(),
        P(),
        P(),
        P(),
        P(),
    )
    out_specs = (P("dom", None), P("dom", None), P(), P(), P(), P(), P(), P())
    return jax.shard_map(body, mesh=mesh, in_specs=in_specs, out_specs=out_specs, check_vma=False)
```
